32 devices in a mesh: particle: 4 (over y, core), tile: 8 (over z, x).
Axes of the slice: x: 2, y: 2, z: 4, core: 2. Of those that a mesh axis runs over, the one named last changes fastest.
Arguments:
- ensemble: float32 [8, 8, 128, 2048], P('particle', None, 'tile'), may hold values from -6 to 6
- owners: int32 [8], replicated, may hold values from 0 to 7, as said below
- velocity_x: float32 [8, 128, 2048], P(None, 'tile'), may hold values from -0.3 to 0.3
- northward_speed_ratio: float32 [8, 128, 2048], P(None, 'tile'), may hold values from -0.3 to 0.3
- target: float32 [8, 128, 2048], P(None, 'tile'), may hold values from -6 to 6
- forcing: bfloat16 [2, 8, 8, 128, 2048], P(None, 'particle', None, 'tile'), may hold values from -6 to 6
- diffusion: float32 [8], replicated, may hold values from 0.05 to 0.2
- nudging: float32 [8], replicated, may hold values from 0.05 to 0.5
- level_depths: float32 [8], replicated, may hold values from 0.25 to 1
Outputs:
- predicted_ensemble_grids: float32 [8, 8, 2048, 128], P('particle', None, 'tile')
- northward_flux_scaled: float32 [8, 2048, 128], P('particle', 'tile')
The draws below stay inside these ranges and needn't reach their ends.
Inputs may be any that keep to these rules, and one draw needn't show every extreme that they name: `owners`: 0 and 7 always occur; other members are copied any number of times.
All inputs are finite; a program needn't handle non-finite values.
Results may differ from the reference program's by a relative error of at most 0.0003.
Values sent between devices are 32-bit elements; how exact they have to be, the bound alone decides.
A program may use at most 128 MiB of HBM per device.

```python
import math
import jax
import jax.numpy as jnp

LAYER_COUNT = 8
NX = 2048
STEPS = 2
MEMBER_COUNT = 8
NY = 128


def draw_owners(key, part):
    first_key = jax.random.fold_in(key, 11)
    second_key = jax.random.fold_in(key, 23)
    shuffled = jax.random.permutation(first_key, jnp.arange(MEMBER_COUNT, dtype=jnp.int32))
    chosen_members = jax.random.randint(second_key, (MEMBER_COUNT,), 0, MEMBER_COUNT, dtype=jnp.int32)
    keeper = (shuffled == 0) | (shuffled == MEMBER_COUNT - 1)
    return jnp.where(keeper, shuffled, chosen_members).astype(jnp.int32)


def block_levels(stream_key, extent, pieces, least, largest):
    def one(axis_at, parts):
        heights = jax.random.uniform(jax.random.fold_in(jax.random.fold_in(stream_key, 6), axis_at), (parts,), jnp.float32, least / len(pieces), largest / len(pieces))
        return jnp.repeat(jnp.exp(heights), extent[axis_at] // parts).reshape((-1,) + (1,) * (len(extent) - axis_at - 1))

    level = one(*pieces[0])
    for cut in pieces[1:]:
        level = level * one(*cut)
    return level


def gaussian(rng, shape, deviation, limit, cuts=(), kind=jnp.bfloat16):
    result = jax.random.normal(rng, shape, jnp.float32) * deviation
    if len(cuts) > 0:
        result = block_levels(rng, shape, cuts, -0.22, 0.18) * result
    return jnp.clip(result, min=-limit, max=limit).astype(kind)


def setup_inputs(seed: int = 0) -> dict:
    seeds = jax.random.split(jax.random.key(seed), 10)
    ensemble = gaussian(seeds[0], (MEMBER_COUNT, LAYER_COUNT, NY, NX), 1.0, 6.0, ((0, 4), (2, 8)), jnp.float32)
    owners = draw_owners(jax.random.fold_in(seeds[9], 71), 0)
    velocity_x = jnp.clip(jax.random.uniform(seeds[2], (LAYER_COUNT, NY, NX), jnp.float32, -0.3, 0.3) * block_levels(seeds[2], (LAYER_COUNT, NY, NX), ((1, 8),), -0.4, 0.0), -0.3, 0.3)
    northward_speed_ratio = jnp.clip(jax.random.uniform(seeds[3], (LAYER_COUNT, NY, NX), jnp.float32, -0.3, 0.3) * block_levels(seeds[3], (LAYER_COUNT, NY, NX), ((1, 8),), -0.4, 0.0), -0.3, 0.3)
    target = gaussian(seeds[4], (LAYER_COUNT, NY, NX), 1.0, 6.0, ((1, 8),), jnp.float32)
    forcing = gaussian(seeds[5], (STEPS, MEMBER_COUNT, LAYER_COUNT, NY, NX), 1.0, 6.0, ((1, 4), (3, 8)))
    diffusion = jnp.clip(jnp.exp(jax.random.uniform(seeds[6], (LAYER_COUNT,), jnp.float32, math.log(0.05), math.log(0.2))), 0.05, 0.2)
    nudging = jnp.clip(jnp.exp(jax.random.uniform(seeds[7], (LAYER_COUNT,), jnp.float32, math.log(0.05), math.log(0.5))), 0.05, 0.5)
    level_depths = jnp.clip(jnp.exp(jax.random.uniform(seeds[8], (LAYER_COUNT,), jnp.float32, math.log(0.25), math.log(1.0))), 0.25, 1.0)
    return dict(ensemble=ensemble, owners=owners, velocity_x=velocity_x, northward_speed_ratio=northward_speed_ratio, target=target, forcing=forcing, diffusion=diffusion, nudging=nudging, level_depths=level_depths)


forcing_scale = 0.5


def advance(padded, velocity_x, northward_speed_ratio, diffusion, nudging, target, forcing_now):
    center = padded[..., 1:-1, :]
    northern = padded[..., 2:, :]
    southern = padded[..., :-2, :]
    eastern = jnp.roll(center, -1, axis=-1)
    west_boundary = jnp.roll(center, 1, axis=-1)
    laplace = eastern + west_boundary + northern + southern - 4.0 * center
    advect = 0.5 * velocity_x * (eastern - west_boundary) + 0.5 * northward_speed_ratio * (northern - southern)
    return (center - advect + diffusion[:, None, None] * laplace
            + nudging[:, None, None] * (target - center)
            + forcing_scale * forcing_now.astype(jnp.float32))


def reference(ensemble, owners, velocity_x, northward_speed_ratio, target, forcing, diffusion, nudging, level_depths):
    prognostic_tracer = jnp.take(ensemble, owners, axis=0)
    for step_index in range(STEPS):
        padded = jnp.pad(prognostic_tracer, ((0, 0), (0, 0), (1, 1), (0, 0)))
        prognostic_tracer = advance(padded, velocity_x, northward_speed_ratio, diffusion, nudging, target, forcing[step_index])
    predicted_ensemble_grids = jnp.transpose(prognostic_tracer, (0, 1, 3, 2))
    vertical_profile = jnp.sum(level_depths[None, :, None, None] * predicted_ensemble_grids, axis=1)
    northward_flux_scaled = jnp.cumsum(vertical_profile, axis=2) * (NY ** -0.5)
    return (predicted_ensemble_grids, northward_flux_scaled)
```

```python
import functools

import jax
import jax.numpy as jnp
from jax import lax
from jax.experimental import pallas as pl
from jax.experimental.pallas import tpu as pltpu
from jax.sharding import PartitionSpec as P

forcing_scale = 0.5
MESH = pl.DeviceIdType.MESH


def fused_cycle(
    groups,
    tiles,
    weight_ref,
    diffusion_ref,
    nudging_ref,
    depth_ref,
    ensemble_ref,
    vx_ref,
    vy_ref,
    target_ref,
    forcing_ref,
    out_ref,
    flux_ref,
    chip_members,
    peer_out,
    peer_in,
    vx,
    vy,
    target,
    forcing,
    padded,
    halo_out,
    halo_in,
    blocks_out,
    blocks_in,
    profile,
    own_sem,
    param_sem,
    sibling_send,
    sibling_recv,
    peer_send,
    peer_recv,
    halo_send,
    halo_recv,
    block_send,
    block_recv,
    block_own,
):
    per_group, levels, rows, columns = ensemble_ref.shape
    steps = forcing_ref.shape[0]
    members = groups * per_group
    chips = groups // 2
    width = columns // tiles
    first = 8
    last = first + rows
    me = lax.axis_index("particle")
    tile = lax.axis_index("tile")
    core = lax.rem(me, 2)
    chip = lax.div(me, 2)
    sibling = me + 1 - 2 * core

    def peer(k):
        return lax.rem(me + 2 * k, groups)

    def other_tile(k):
        return lax.rem(tile + k, tiles)

    params = [
        pltpu.make_async_copy(src, dst, param_sem.at[i])
        for i, (src, dst) in enumerate(
            [(vx_ref, vx), (vy_ref, vy), (target_ref, target), (forcing_ref, forcing)]
        )
    ]

    def own_copy(level):
        return pltpu.make_async_copy(
            ensemble_ref.at[:, level], chip_members.at[core, level], own_sem.at[level]
        )

    def sibling_copy(level):
        return pltpu.make_async_remote_copy(
            src_ref=ensemble_ref.at[:, level],
            dst_ref=chip_members.at[core, level],
            send_sem=sibling_send.at[level],
            recv_sem=sibling_recv.at[level],
            device_id=(sibling, tile),
            device_id_type=MESH,
        )

    def sibling_arrival(level):
        return pltpu.make_async_remote_copy(
            src_ref=ensemble_ref.at[:, level],
            dst_ref=chip_members.at[1 - core, level],
            send_sem=sibling_send.at[level],
            recv_sem=sibling_recv.at[level],
            device_id=(sibling, tile),
            device_id_type=MESH,
        )

    def peer_copy(level, k):
        return pltpu.make_async_remote_copy(
            src_ref=peer_out.at[level, k - 1],
            dst_ref=peer_in.at[level, k - 1],
            send_sem=peer_send.at[level, k - 1],
            recv_sem=peer_recv.at[level, k - 1],
            device_id=(peer(k), tile),
            device_id_type=MESH,
        )

    def halo_copy(step, level, side):
        return pltpu.make_async_remote_copy(
            src_ref=halo_out.at[step, level, side],
            dst_ref=halo_in.at[step, level, side],
            send_sem=halo_send.at[step, level, side],
            recv_sem=halo_recv.at[step, level, side],
            device_id=(me, tile + 1 - 2 * side),
            device_id_type=MESH,
        )

    def block_copy(level, k):
        return pltpu.make_async_remote_copy(
            src_ref=blocks_out.at[level, other_tile(k)],
            dst_ref=blocks_in.at[level, tile],
            send_sem=block_send.at[level, k],
            recv_sem=block_recv.at[level, k],
            device_id=(me, other_tile(k)),
            device_id_type=MESH,
        )

    def block_arrival(level, k):
        return pltpu.make_async_remote_copy(
            src_ref=blocks_out.at[level, other_tile(k)],
            dst_ref=blocks_in.at[level, other_tile(tiles - k)],
            send_sem=block_send.at[level, k],
            recv_sem=block_recv.at[level, k],
            device_id=(me, other_tile(k)),
            device_id_type=MESH,
        )

    def block_stay(level):
        return pltpu.make_async_copy(
            blocks_out.at[level, tile], blocks_in.at[level, tile], block_own.at[level]
        )

    def from_chip(level, slot):
        total = None
        for c in range(2):
            for j in range(per_group):
                w = weight_ref[slot * members + chip * (2 * per_group) + c * per_group + j]
                term = w * chip_members[c, level, j]
                total = term if total is None else total + term
        return total

    def send_halo(step, level):
        for j in range(per_group):
            halo_out[step, level, 0, j : j + 1, :] = padded[step, level, j, last - 1 : last, :]
            halo_out[step, level, 1, j : j + 1, :] = padded[step, level, j, first : first + 1, :]

        @pl.when(tile < tiles - 1)
        def _():
            halo_copy(step, level, 0).start()

        @pl.when(tile > 0)
        def _():
            halo_copy(step, level, 1).start()

    def take_halo(step, level):
        zero = jnp.zeros((1, columns), jnp.float32)

        @pl.when(tile > 0)
        def _():
            halo_copy(step, level, 0).wait_recv()
            for j in range(per_group):
                padded[step, level, j, first - 1 : first, :] = halo_in[step, level, 0, j : j + 1, :]

        @pl.when(tile == 0)
        def _():
            for j in range(per_group):
                padded[step, level, j, first - 1 : first, :] = zero

        @pl.when(tile < tiles - 1)
        def _():
            halo_copy(step, level, 1).wait_recv()
            for j in range(per_group):
                padded[step, level, j, last : last + 1, :] = halo_in[step, level, 1, j : j + 1, :]

        @pl.when(tile == tiles - 1)
        def _():
            for j in range(per_group):
                padded[step, level, j, last : last + 1, :] = zero

    def advance(step, level, j):
        d = diffusion_ref[level]
        g = nudging_ref[level]
        hx = 0.5 * vx[level]
        hy = 0.5 * vy[level]
        center = padded[step, level, j, first:last, :]
        north = padded[step, level, j, first + 1 : last + 1, :]
        south = padded[step, level, j, first - 1 : last - 1, :]
        east = pltpu.roll(center, columns - 1, 1)
        west = pltpu.roll(center, 1, 1)
        return (
            (1.0 - 4.0 * d - g) * center
            + (d - hx) * east
            + (d + hx) * west
            + (d - hy) * north
            + (d + hy) * south
            + g * target[level]
            + forcing_scale * forcing[step, j, level].astype(jnp.float32)
        )

    barrier = pltpu.get_barrier_semaphore()
    partners = [(sibling, tile)]
    partners += [(peer(k), tile) for k in range(1, chips)]
    partners += [(me, other_tile(k)) for k in range(1, tiles)]
    for partner in partners:
        pl.semaphore_signal(barrier, inc=1, device_id=partner, device_id_type=MESH)
    for level in range(levels):
        own_copy(level).start()
    for copy in params:
        copy.start()
    pl.semaphore_wait(barrier, len(partners))

    @pl.loop(0, levels)
    def _(level):
        sibling_copy(level).start()

    @pl.loop(0, levels)
    def _(level):
        own_copy(level).wait()
        sibling_arrival(level).wait_recv()
        for k in range(1, chips):
            for j in range(per_group):
                peer_out[level, k - 1, j] = from_chip(level, peer(k) * per_group + j)
            peer_copy(level, k).start()

    for copy in params:
        copy.wait()

    @pl.loop(0, levels + steps)
    def _(turn):
        @pl.when(turn < levels)
        def _():
            level = turn
            for k in range(1, chips):
                peer_copy(level, k).wait_recv()
            for j in range(per_group):
                value = from_chip(level, me * per_group + j)
                for k in range(1, chips):
                    value = value + peer_in[level, k - 1, j]
                padded[0, level, j, first:last, :] = value
            send_halo(0, level)

        for step in range(steps):

            @pl.when((turn >= step + 1) & (turn < levels + step + 1))
            def _():
                level = turn - step - 1
                take_halo(step, level)
                for j in range(per_group):
                    value = advance(step, level, j)
                    if step + 1 < steps:
                        padded[step + 1, level, j, first:last, :] = value
                    else:
                        for t in range(tiles):
                            blocks_out[level, t, j] = value[:, t * width : (t + 1) * width]
                if step + 1 < steps:
                    send_halo(step + 1, level)
                else:
                    block_stay(level).start()
                    for k in range(1, tiles):
                        block_copy(level, k).start()

    profile[...] = jnp.zeros_like(profile)

    @pl.loop(0, levels)
    def _(level):
        block_stay(level).wait()
        for k in range(1, tiles):
            block_arrival(level, k).wait_recv()
        for j in range(per_group):
            whole = blocks_in[level, :, j].reshape(tiles * rows, width)
            turned = whole.T
            out_ref[j, level] = turned
            profile[j] = profile[j] + depth_ref[level] * turned

    extent = tiles * rows
    row = lax.broadcasted_iota(jnp.int32, (extent, extent), 0)
    upto = lax.broadcasted_iota(jnp.int32, (extent, extent), 1)
    mask = (row <= upto).astype(jnp.float32)
    for j in range(per_group):
        flux_ref[j] = jnp.dot(
            profile[j],
            mask,
            precision=lax.Precision.HIGHEST,
            preferred_element_type=jnp.float32,
        ) * extent ** (-0.5)

    @pl.loop(0, levels)
    def _(level):
        sibling_copy(level).wait_send()
        for k in range(1, chips):
            peer_copy(level, k).wait_send()
        for step in range(steps):

            @pl.when(tile < tiles - 1)
            def _():
                halo_copy(step, level, 0).wait_send()

            @pl.when(tile > 0)
            def _():
                halo_copy(step, level, 1).wait_send()

        for k in range(1, tiles):
            block_copy(level, k).wait_send()


def with_kernel(
    groups, tiles, ensemble, owners, velocity_x, velocity_y, target, forcing, diffusion, nudging, depths
):
    per_group, levels, rows, columns = ensemble.shape
    steps = forcing.shape[0]
    members = groups * per_group
    peers = max(groups // 2 - 1, 1)
    width = columns // tiles
    weights = (owners[:, None] == jnp.arange(members, dtype=owners.dtype)[None, :]).astype(jnp.float32)
    f32 = jnp.float32
    dma = pltpu.SemaphoreType.DMA
    smem = pl.BlockSpec(memory_space=pltpu.SMEM)
    anywhere = pl.BlockSpec(memory_space=pl.ANY)
    vmem = pl.BlockSpec(memory_space=pltpu.VMEM)
    points = levels * per_group * rows * columns
    return pl.pallas_call(
        functools.partial(fused_cycle, groups, tiles),
        out_shape=(
            jax.ShapeDtypeStruct((per_group, levels, width, tiles * rows), f32),
            jax.ShapeDtypeStruct((per_group, width, tiles * rows), f32),
        ),
        in_specs=[smem] * 4 + [anywhere] * 5,
        out_specs=(vmem, vmem),
        scratch_shapes=[
            pltpu.VMEM((2, levels, per_group, rows, columns), f32),
            pltpu.VMEM((levels, peers, per_group, rows, columns), f32),
            pltpu.VMEM((levels, peers, per_group, rows, columns), f32),
            pltpu.VMEM(velocity_x.shape, f32),
            pltpu.VMEM(velocity_y.shape, f32),
            pltpu.VMEM(target.shape, f32),
            pltpu.VMEM(forcing.shape, forcing.dtype),
            pltpu.VMEM((steps, levels, per_group, rows + 16, columns), f32),
            pltpu.VMEM((steps, levels, 2, per_group, columns), f32),
            pltpu.VMEM((steps, levels, 2, per_group, columns), f32),
            pltpu.VMEM((levels, tiles, per_group, rows, width), f32),
            pltpu.VMEM((levels, tiles, per_group, rows, width), f32),
            pltpu.VMEM((per_group, width, tiles * rows), f32),
            dma((levels,)),
            dma((4,)),
            dma((levels,)),
            dma((levels,)),
            dma((levels, peers)),
            dma((levels, peers)),
            dma((steps, levels, 2)),
            dma((steps, levels, 2)),
            dma((levels, tiles)),
            dma((levels, tiles)),
            dma((levels,)),
        ],
        compiler_params=pltpu.CompilerParams(
            collective_id=0, has_side_effects=True, vmem_limit_bytes=56 * 1024 * 1024
        ),
        cost_estimate=pl.CostEstimate(
            flops=points * steps * 14, bytes_accessed=points * 20, transcendentals=0
        ),
    )(
        weights.reshape(-1),
        diffusion,
        nudging,
        depths,
        ensemble,
        velocity_x,
        velocity_y,
        target,
        forcing,
    )


def gather_groups(value, axis):
    size = lax.axis_size(axis)
    me = lax.axis_index(axis)
    parts = [value]
    for k in range(1, size):
        parts.append(lax.ppermute(value, axis, [((i + k) % size, i) for i in range(size)]))
    stacked = jnp.concatenate(parts, axis=0)
    return jnp.roll(stacked, me * value.shape[0], axis=0)


def with_halo(value, axis, dim):
    size, length = (lax.axis_size(axis), value.shape[dim])
    up = [(i, (i + 1) % size) for i in range(size - 1)]
    down = [(j, i) for i, j in up]
    before = lax.ppermute(lax.slice_in_dim(value, length - 1, length, axis=dim), axis, up)
    after = lax.ppermute(lax.slice_in_dim(value, 0, 1, axis=dim), axis, down)
    return jnp.concatenate([before, value, after], axis=dim)


def advance_whole(padded, velocity_x, velocity_y, diffusion, nudging, target, forcing_now):
    center = padded[..., 1:-1, :]
    northern = padded[..., 2:, :]
    southern = padded[..., :-2, :]
    eastern = jnp.roll(center, -1, axis=-1)
    western = jnp.roll(center, 1, axis=-1)
    laplace = eastern + western + northern + southern - 4.0 * center
    advect = 0.5 * velocity_x * (eastern - western) + 0.5 * velocity_y * (northern - southern)
    return (
        center
        - advect
        + diffusion[:, None, None] * laplace
        + nudging[:, None, None] * (target - center)
        + forcing_scale * forcing_now.astype(jnp.float32)
    )


def with_collectives(
    ensemble, owners, velocity_x, velocity_y, target, forcing, diffusion, nudging, depths
):
    per_group = ensemble.shape[0]
    wanted = lax.dynamic_slice_in_dim(owners, lax.axis_index("particle") * per_group, per_group)
    gathered = gather_groups(ensemble, "particle")
    candidates = jnp.arange(gathered.shape[0], dtype=owners.dtype)
    matches = (wanted[:, None] == candidates[None, :]).astype(jnp.float32)
    field = jnp.einsum("jk,klrx->jlrx", matches, gathered, precision=lax.Precision.HIGHEST)
    for step in range(forcing.shape[0]):
        padded = with_halo(field, "tile", 2)
        field = advance_whole(
            padded, velocity_x, velocity_y, diffusion, nudging, target, forcing[step]
        )
    turned = jnp.transpose(field, (0, 1, 3, 2))
    arrived = lax.all_to_all(turned, "tile", split_axis=2, concat_axis=3, tiled=True)
    profile = jnp.sum(depths[None, :, None, None] * arrived, axis=1)
    extent = arrived.shape[3]
    upto = jnp.triu(jnp.ones((extent, extent), jnp.float32))
    flux = jnp.einsum("pxr,ry->pxy", profile, upto, precision=lax.Precision.HIGHEST)
    return (arrived, flux * extent ** (-0.5))


def on_device(groups, tiles, ensemble, *others):
    rows, columns = ensemble.shape[2:]
    aligned = columns % (tiles * 128) == 0 and rows % 16 == 0 and (tiles * rows) % 128 == 0
    if aligned and groups % 2 == 0 and groups > 2:
        return with_kernel(groups, tiles, ensemble, *others)
    return with_collectives(ensemble, *others)


def solution(mesh):
    placed = (
        P("particle", None, "tile", None),
        P(),
        P(None, "tile", None),
        P(None, "tile", None),
        P(None, "tile", None),
        P(None, "particle", None, "tile", None),
        P(),
        P(),
        P(),
    )
    return jax.shard_map(
        functools.partial(on_device, mesh.shape["particle"], mesh.shape["tile"]),
        mesh=mesh,
        in_specs=placed,
        out_specs=(P("particle", None, "tile", None), P("particle", "tile", None)),
        check_vma=False,
    )
```

```python
import functools

import jax
import jax.numpy as jnp
from jax import lax
from jax.experimental import pallas as pl
from jax.experimental.pallas import tpu as pltpu
from jax.sharding import PartitionSpec as P

forcing_scale = 0.5
MESH = pl.DeviceIdType.MESH


def fused_cycle(
    groups,
    tiles,
    owners_ref,
    diffusion_ref,
    nudging_ref,
    depth_ref,
    ensemble_ref,
    vx_ref,
    vy_ref,
    target_ref,
    forcing_ref,
    out_ref,
    flux_ref,
    chip_members,
    peer_out,
    peer_in,
    vx,
    vy,
    target,
    forcing,
    padded,
    halo_out,
    halo_in,
    blocks_out,
    blocks_in,
    turned,
    profile,
    own_sem,
    param_sem,
    sibling_send,
    sibling_recv,
    peer_send,
    peer_recv,
    halo_send,
    halo_recv,
    block_send,
    block_recv,
    block_own,
    out_sem,
):
    per_group, levels, rows, columns = ensemble_ref.shape
    steps = forcing_ref.shape[0]
    chips = groups // 2
    width = columns // tiles
    first = 8
    last = first + rows
    gap = 1
    pieces = levels * per_group
    me = lax.axis_index("particle")
    tile = lax.axis_index("tile")
    core = lax.rem(me, 2)
    chip = lax.div(me, 2)
    sibling = me + 1 - 2 * core

    def peer(k):
        return lax.rem(me + 2 * k, groups)

    def other_tile(k):
        return lax.rem(tile + k, tiles)

    params = [
        pltpu.make_async_copy(src, dst, param_sem.at[i])
        for i, (src, dst) in enumerate(
            [(vx_ref, vx), (vy_ref, vy), (target_ref, target), (forcing_ref, forcing)]
        )
    ]

    def own_copy(level):
        return pltpu.make_async_copy(
            ensemble_ref.at[:, level], chip_members.at[core, level], own_sem.at[level]
        )

    def sibling_copy(level):
        return pltpu.make_async_remote_copy(
            src_ref=ensemble_ref.at[:, level],
            dst_ref=chip_members.at[core, level],
            send_sem=sibling_send.at[level],
            recv_sem=sibling_recv.at[level],
            device_id=(sibling, tile),
            device_id_type=MESH,
        )

    def sibling_arrival(level):
        return pltpu.make_async_remote_copy(
            src_ref=ensemble_ref.at[:, level],
            dst_ref=chip_members.at[1 - core, level],
            send_sem=sibling_send.at[level],
            recv_sem=sibling_recv.at[level],
            device_id=(sibling, tile),
            device_id_type=MESH,
        )

    def peer_copy(piece, k):
        return pltpu.make_async_remote_copy(
            src_ref=peer_out.at[piece, k - 1],
            dst_ref=peer_in.at[piece, k - 1],
            send_sem=peer_send.at[piece, k - 1],
            recv_sem=peer_recv.at[piece, k - 1],
            device_id=(peer(k), tile),
            device_id_type=MESH,
        )

    def halo_copy(step, piece, side):
        return pltpu.make_async_remote_copy(
            src_ref=halo_out.at[step, piece, side],
            dst_ref=halo_in.at[step, piece, side],
            send_sem=halo_send.at[step, piece, side],
            recv_sem=halo_recv.at[step, piece, side],
            device_id=(me, tile + 1 - 2 * side),
            device_id_type=MESH,
        )

    def block_copy(piece, k):
        return pltpu.make_async_remote_copy(
            src_ref=blocks_out.at[piece, other_tile(k)],
            dst_ref=blocks_in.at[piece, tile],
            send_sem=block_send.at[piece, k],
            recv_sem=block_recv.at[piece, k],
            device_id=(me, other_tile(k)),
            device_id_type=MESH,
        )

    def block_arrival(piece, k):
        return pltpu.make_async_remote_copy(
            src_ref=blocks_out.at[piece, other_tile(k)],
            dst_ref=blocks_in.at[piece, other_tile(tiles - k)],
            send_sem=block_send.at[piece, k],
            recv_sem=block_recv.at[piece, k],
            device_id=(me, other_tile(k)),
            device_id_type=MESH,
        )

    def block_stay(piece):
        return pltpu.make_async_copy(
            blocks_out.at[piece, tile], blocks_in.at[piece, tile], block_own.at[piece]
        )

    def out_copy(piece):
        return pltpu.make_async_copy(turned.at[piece], out_ref.at[lax.rem(piece, per_group), lax.div(piece, per_group)], out_sem.at[piece])

    def from_chip(level, slot):
        owner = owners_ref[slot]
        total = None
        for c in range(2):
            for j in range(per_group):
                member = chip * (2 * per_group) + c * per_group + j
                w = (owner == member).astype(jnp.float32)
                term = w * chip_members[c, level, j]
                total = term if total is None else total + term
        return total

    def send_halo(step, piece):
        halo_out[step, piece, 0] = padded[step, piece, last - 1 : last, :]
        halo_out[step, piece, 1] = padded[step, piece, first : first + 1, :]

        @pl.when(tile < tiles - 1)
        def _():
            halo_copy(step, piece, 0).start()

        @pl.when(tile > 0)
        def _():
            halo_copy(step, piece, 1).start()

    def take_halo(step, piece):
        zero = jnp.zeros((1, columns), jnp.float32)

        @pl.when(tile > 0)
        def _():
            halo_copy(step, piece, 0).wait_recv()
            padded[step, piece, first - 1 : first, :] = halo_in[step, piece, 0]

        @pl.when(tile == 0)
        def _():
            padded[step, piece, first - 1 : first, :] = zero

        @pl.when(tile < tiles - 1)
        def _():
            halo_copy(step, piece, 1).wait_recv()
            padded[step, piece, last : last + 1, :] = halo_in[step, piece, 1]

        @pl.when(tile == tiles - 1)
        def _():
            padded[step, piece, last : last + 1, :] = zero

    def advance(step, piece):
        level = lax.div(piece, per_group)
        j = lax.rem(piece, per_group)
        d = diffusion_ref[level]
        g = nudging_ref[level]
        hx = 0.5 * vx[level]
        hy = 0.5 * vy[level]
        center = padded[step, piece, first:last, :]
        north = padded[step, piece, first + 1 : last + 1, :]
        south = padded[step, piece, first - 1 : last - 1, :]
        east = pltpu.roll(center, columns - 1, 1)
        west = pltpu.roll(center, 1, 1)
        return (
            (1.0 - 4.0 * d - g) * center
            + (d - hx) * east
            + (d + hx) * west
            + (d - hy) * north
            + (d + hy) * south
            + g * target[level]
            + forcing_scale * forcing[step, j, level].astype(jnp.float32)
        )

    barrier = pltpu.get_barrier_semaphore()
    partners = [(sibling, tile)]
    partners += [(peer(k), tile) for k in range(1, chips)]
    partners += [(me, other_tile(k)) for k in range(1, tiles)]
    for partner in partners:
        pl.semaphore_signal(barrier, inc=1, device_id=partner, device_id_type=MESH)
    for level in range(levels):
        own_copy(level).start()
    pl.semaphore_wait(barrier, len(partners))

    @pl.loop(0, levels)
    def _(level):
        sibling_copy(level).start()

    for copy in params:
        copy.start()

    @pl.loop(0, levels)
    def _(level):
        own_copy(level).wait()
        sibling_arrival(level).wait_recv()
        for j in range(per_group):
            for k in range(1, chips):
                piece = level * per_group + j
                peer_out[piece, k - 1] = from_chip(level, peer(k) * per_group + j)
                peer_copy(piece, k).start()

    for copy in params:
        copy.wait()

    @pl.loop(0, pieces + gap * steps)
    def _(turn):
        @pl.when(turn < pieces)
        def _():
            piece = turn
            for k in range(1, chips):
                peer_copy(piece, k).wait_recv()
            value = from_chip(
                lax.div(piece, per_group), me * per_group + lax.rem(piece, per_group)
            )
            for k in range(1, chips):
                value = value + peer_in[piece, k - 1]
            padded[0, piece, first:last, :] = value
            send_halo(0, piece)

        for step in range(steps):

            @pl.when((turn >= gap * (step + 1)) & (turn < pieces + gap * (step + 1)))
            def _():
                piece = turn - gap * (step + 1)
                take_halo(step, piece)
                value = advance(step, piece)
                if step + 1 < steps:
                    padded[step + 1, piece, first:last, :] = value
                    send_halo(step + 1, piece)
                else:
                    for t in range(tiles):
                        blocks_out[piece, t] = value[:, t * width : (t + 1) * width]
                    block_stay(piece).start()
                    for k in sorted(range(1, tiles), key=lambda k: abs(k - tiles // 2)):
                        block_copy(piece, k).start()

    profile[...] = jnp.zeros_like(profile)

    @pl.loop(0, levels)
    def _(level):
        for j in range(per_group):
            piece = level * per_group + j
            block_stay(piece).wait()
            for k in range(1, tiles):
                block_arrival(piece, k).wait_recv()
            columns_first = blocks_in[piece].reshape(tiles * rows, width).T
            turned[piece] = columns_first
            profile[j] = profile[j] + depth_ref[level] * columns_first
            out_copy(piece).start()

    extent = tiles * rows
    row = lax.broadcasted_iota(jnp.int32, (extent, extent), 0)
    upto = lax.broadcasted_iota(jnp.int32, (extent, extent), 1)
    mask = (row <= upto).astype(jnp.float32)
    for j in range(per_group):
        flux_ref[j] = jnp.dot(
            profile[j],
            mask,
            precision=lax.Precision.HIGHEST,
            preferred_element_type=jnp.float32,
        ) * extent ** (-0.5)

    @pl.loop(0, levels)
    def _(level):
        sibling_copy(level).wait_send()

    @pl.loop(0, pieces)
    def _(piece):
        out_copy(piece).wait()
        for k in range(1, chips):
            peer_copy(piece, k).wait_send()
        for step in range(steps):

            @pl.when(tile < tiles - 1)
            def _():
                halo_copy(step, piece, 0).wait_send()

            @pl.when(tile > 0)
            def _():
                halo_copy(step, piece, 1).wait_send()

        for k in range(1, tiles):
            block_copy(piece, k).wait_send()


def with_kernel(
    groups, tiles, ensemble, owners, velocity_x, velocity_y, target, forcing, diffusion, nudging, depths
):
    per_group, levels, rows, columns = ensemble.shape
    steps = forcing.shape[0]
    peers = max(groups // 2 - 1, 1)
    width = columns // tiles
    f32 = jnp.float32
    dma = pltpu.SemaphoreType.DMA
    smem = pl.BlockSpec(memory_space=pltpu.SMEM)
    anywhere = pl.BlockSpec(memory_space=pl.ANY)
    vmem = pl.BlockSpec(memory_space=pltpu.VMEM)
    pieces = levels * per_group
    points = levels * per_group * rows * columns
    return pl.pallas_call(
        functools.partial(fused_cycle, groups, tiles),
        out_shape=(
            jax.ShapeDtypeStruct((per_group, levels, width, tiles * rows), f32),
            jax.ShapeDtypeStruct((per_group, width, tiles * rows), f32),
        ),
        in_specs=[smem] * 4 + [anywhere] * 5,
        out_specs=(anywhere, vmem),
        scratch_shapes=[
            pltpu.VMEM((2, levels, per_group, rows, columns), f32),
            pltpu.VMEM((pieces, peers, rows, columns), f32),
            pltpu.VMEM((pieces, peers, rows, columns), f32),
            pltpu.VMEM(velocity_x.shape, f32),
            pltpu.VMEM(velocity_y.shape, f32),
            pltpu.VMEM(target.shape, f32),
            pltpu.VMEM(forcing.shape, forcing.dtype),
            pltpu.VMEM((steps, pieces, rows + 16, columns), f32),
            pltpu.VMEM((steps, pieces, 2, 1, columns), f32),
            pltpu.VMEM((steps, pieces, 2, 1, columns), f32),
            pltpu.VMEM((pieces, tiles, rows, width), f32),
            pltpu.VMEM((pieces, tiles, rows, width), f32),
            pltpu.VMEM((pieces, width, tiles * rows), f32),
            pltpu.VMEM((per_group, width, tiles * rows), f32),
            dma((levels,)),
            dma((4,)),
            dma((levels,)),
            dma((levels,)),
            dma((pieces, peers)),
            dma((pieces, peers)),
            dma((steps, pieces, 2)),
            dma((steps, pieces, 2)),
            dma((pieces, tiles)),
            dma((pieces, tiles)),
            dma((pieces,)),
            dma((pieces,)),
        ],
        compiler_params=pltpu.CompilerParams(
            collective_id=0, has_side_effects=True, vmem_limit_bytes=56 * 1024 * 1024
        ),
        cost_estimate=pl.CostEstimate(
            flops=points * steps * 14, bytes_accessed=points * 20, transcendentals=0
        ),
    )(
        owners,
        diffusion,
        nudging,
        depths,
        ensemble,
        velocity_x,
        velocity_y,
        target,
        forcing,
    )


def gather_groups(value, axis):
    size = lax.axis_size(axis)
    me = lax.axis_index(axis)
    parts = [value]
    for k in range(1, size):
        parts.append(lax.ppermute(value, axis, [((i + k) % size, i) for i in range(size)]))
    stacked = jnp.concatenate(parts, axis=0)
    return jnp.roll(stacked, me * value.shape[0], axis=0)


def with_halo(value, axis, dim):
    size, length = (lax.axis_size(axis), value.shape[dim])
    up = [(i, (i + 1) % size) for i in range(size - 1)]
    down = [(j, i) for i, j in up]
    before = lax.ppermute(lax.slice_in_dim(value, length - 1, length, axis=dim), axis, up)
    after = lax.ppermute(lax.slice_in_dim(value, 0, 1, axis=dim), axis, down)
    return jnp.concatenate([before, value, after], axis=dim)


def advance_whole(padded, velocity_x, velocity_y, diffusion, nudging, target, forcing_now):
    center = padded[..., 1:-1, :]
    northern = padded[..., 2:, :]
    southern = padded[..., :-2, :]
    eastern = jnp.roll(center, -1, axis=-1)
    western = jnp.roll(center, 1, axis=-1)
    laplace = eastern + western + northern + southern - 4.0 * center
    advect = 0.5 * velocity_x * (eastern - western) + 0.5 * velocity_y * (northern - southern)
    return (
        center
        - advect
        + diffusion[:, None, None] * laplace
        + nudging[:, None, None] * (target - center)
        + forcing_scale * forcing_now.astype(jnp.float32)
    )


def with_collectives(
    ensemble, owners, velocity_x, velocity_y, target, forcing, diffusion, nudging, depths
):
    per_group = ensemble.shape[0]
    wanted = lax.dynamic_slice_in_dim(owners, lax.axis_index("particle") * per_group, per_group)
    gathered = gather_groups(ensemble, "particle")
    candidates = jnp.arange(gathered.shape[0], dtype=owners.dtype)
    matches = (wanted[:, None] == candidates[None, :]).astype(jnp.float32)
    field = jnp.einsum("jk,klrx->jlrx", matches, gathered, precision=lax.Precision.HIGHEST)
    for step in range(forcing.shape[0]):
        padded = with_halo(field, "tile", 2)
        field = advance_whole(
            padded, velocity_x, velocity_y, diffusion, nudging, target, forcing[step]
        )
    turned = jnp.transpose(field, (0, 1, 3, 2))
    arrived = lax.all_to_all(turned, "tile", split_axis=2, concat_axis=3, tiled=True)
    profile = jnp.sum(depths[None, :, None, None] * arrived, axis=1)
    extent = arrived.shape[3]
    upto = jnp.triu(jnp.ones((extent, extent), jnp.float32))
    flux = jnp.einsum("pxr,ry->pxy", profile, upto, precision=lax.Precision.HIGHEST)
    return (arrived, flux * extent ** (-0.5))


def on_device(groups, tiles, ensemble, *others):
    rows, columns = ensemble.shape[2:]
    aligned = columns % (tiles * 128) == 0 and rows % 16 == 0 and (tiles * rows) % 128 == 0
    if aligned and groups % 2 == 0 and groups > 2:
        return with_kernel(groups, tiles, ensemble, *others)
    return with_collectives(ensemble, *others)


def solution(mesh):
    placed = (
        P("particle", None, "tile", None),
        P(),
        P(None, "tile", None),
        P(None, "tile", None),
        P(None, "tile", None),
        P(None, "particle", None, "tile", None),
        P(),
        P(),
        P(),
    )
    return jax.shard_map(
        functools.partial(on_device, mesh.shape["particle"], mesh.shape["tile"]),
        mesh=mesh,
        in_specs=placed,
        out_specs=(P("particle", None, "tile", None), P("particle", "tile", None)),
        check_vma=False,
    )
```
